512 devices in a mesh: tm: 8 (over z_lo, x), tile: 64 (over y, z_hi, core).
Axes of the slice: x: 4, y: 8, z: 8 (z_hi: 4, z_lo: 2; z = z_hi * 2 + z_lo), core: 2. Of those that a mesh axis runs over, the one named last changes fastest.
Arguments:
- inputs: bfloat16 [16, 64, 24576], P('tm', 'tile'), may hold values from -80 to 80
- cotangent: bfloat16 [16, 64, 24576], P('tm', 'tile'), may hold values from -6 to 6
- frame_weight: int32 [16], P('tm'), may hold values from 1 to 4
- gain_one: float32 [192], replicated, may hold values from 0.1 to 1.9
- conv_one: bfloat16 [3, 3, 3, 192, 192], replicated, may hold values from -0.078125 to 0.078125
- gain_two: float32 [192], replicated, may hold values from 0.1 to 1.9
- conv_two: bfloat16 [3, 3, 3, 192, 192], replicated, may hold values from -0.078125 to 0.078125
Outputs:
- input_grad: bfloat16 [16, 64, 24576], P('tm', None, 'tile')
The draws below stay inside these ranges and needn't reach their ends.
All inputs are finite; a program needn't handle non-finite values.
Results may differ from the reference program's by a relative error of at most 0.0059.
Values may be sent and summed in bfloat16 or wider, within the bound.
No kernel may reach another device: no remote copies, remote signals or barrier semaphores. Data moves between devices by JAX's collectives and lax.ppermute only.
A program may use at most 128 MiB of HBM per device.

```python
import jax
import jax.numpy as jnp
from jax import lax

CHANNELS = 192
COLS = 128
FRAMES = 16
ROWS = 64


def draw_inputs(key, part):
    key = jax.random.fold_in(key, 11)
    first, second, third = jax.random.split(key, 3)
    shape = (FRAMES, ROWS, COLS, CHANNELS)
    base = jnp.clip(jax.random.normal(first, shape, jnp.float32), -4.0, 4.0)
    cell = 10.0 ** jax.random.uniform(second, (FRAMES, ROWS, COLS, 1), jnp.float32)
    channel = 2.0 ** jax.random.uniform(third, (CHANNELS,), jnp.float32, -1.0, 1.0)
    return (base * cell * channel).reshape(FRAMES, ROWS, COLS * CHANNELS).astype(jnp.bfloat16)


def with_ends(entries, own_key, low, largest):
    shape = entries.shape
    index_at = [jax.random.randint(jax.random.fold_in(own_key, axis), (), 0, shape[axis]) for axis in range(len(shape))]
    entries = entries.at[tuple(index_at)].set(low)
    longest = shape.index(max(shape))
    index_at[longest] = (index_at[longest] + 1) % shape[longest]
    return entries.at[tuple(index_at)].set(largest)


def shard_levels(own_key, extent, shards, least, high):
    loudness = 1.0
    for axis_at, blocks in shards:
        heights = jax.random.uniform(jax.random.fold_in(jax.random.fold_in(own_key, 6), axis_at), (blocks,), jnp.float32, least / len(shards), high / len(shards))
        loudness = loudness * jnp.repeat(jnp.exp(heights), extent[axis_at] // blocks).reshape((-1,) + (1,) * (len(extent) - 1 - axis_at))
    return loudness


def normal_values(own_key, shape, scale, reach, pieces=(), kind=jnp.bfloat16):
    array = jax.random.normal(own_key, shape, jnp.float32) * scale
    if len(pieces) > 0:
        array = shard_levels(own_key, shape, pieces, -0.22, 0.18) * array
    return jnp.clip(array, min=-reach, max=reach).astype(kind)


def setup_inputs(seed: int = 0) -> dict:
    arg_keys = jax.random.split(jax.random.key(seed), 8)
    inputs = draw_inputs(jax.random.fold_in(arg_keys[7], 71), 0)
    cotangent = normal_values(arg_keys[1], (FRAMES, ROWS, COLS * CHANNELS), 1.0, 6.0, ((0, 8), (1, 64)))
    frame_weight = with_ends(jax.random.randint(arg_keys[2], (FRAMES,), 1, 5), jax.random.fold_in(arg_keys[2], 1), 1, 4).astype(jnp.int32)
    gain_one = jnp.clip(1.0 + 0.18 * jax.random.normal(arg_keys[3], (CHANNELS,), jnp.float32), 0.1, 1.9)
    conv_one = normal_values(arg_keys[4], (3, 3, 3, CHANNELS, CHANNELS), (27 * CHANNELS) ** -0.5, 0.078125)
    gain_two = jnp.clip(1.0 + 0.18 * jax.random.normal(arg_keys[5], (CHANNELS,), jnp.float32), 0.1, 1.9)
    conv_two = normal_values(arg_keys[6], (3, 3, 3, CHANNELS, CHANNELS), (27 * CHANNELS) ** -0.5, 0.078125)
    return {"inputs": inputs, "cotangent": cotangent, "frame_weight": frame_weight, "gain_one": gain_one, "conv_one": conv_one, "gain_two": gain_two, "conv_two": conv_two}


EPS = 1e-06

def correlate(padded, kern, frames, rows, cols):
    outward = kern.shape[-1]
    total = jnp.zeros((frames * rows * cols, outward), jnp.float32)
    for a in range(3):
        for b in range(3):
            taps = jnp.concatenate([padded[a:a + frames, b:b + rows, e:e + cols] for e in range(3)], axis=-1)
            total = total + jnp.dot(taps.reshape(frames * rows * cols, -1), kern[a, b].reshape(-1, outward), preferred_element_type=jnp.float32)
    return total.reshape(frames, rows, cols, outward)

def norm_back(value, gain, grad):
    scale = lax.rsqrt(lax.optimization_barrier(jnp.mean(value * value, axis=-1, keepdims=True)) + EPS)
    normed = value * scale
    act = normed * gain
    sig = jax.nn.sigmoid(act)
    d_norm = grad * sig * (1.0 + act * (1.0 - sig)) * gain
    return scale * (d_norm - normed * lax.optimization_barrier(jnp.mean(d_norm * normed, axis=-1, keepdims=True)))

def reference(inputs, cotangent, frame_weight, gain_one, conv_one, gain_two, conv_two):
    frames, rows, merged = inputs.shape
    width = gain_one.shape[0]
    cols = merged // width
    values = inputs.reshape(frames, rows, cols, width).astype(jnp.float32)
    scale = lax.rsqrt(lax.optimization_barrier(jnp.mean(values * values, axis=-1, keepdims=True)) + EPS)
    hidden = jax.nn.silu(values * scale * gain_one).astype(jnp.bfloat16)
    z_one = correlate(jnp.pad(hidden, ((2, 0), (1, 1), (1, 1), (0, 0))), conv_one, frames, rows, cols)
    weighted = frame_weight.astype(jnp.float32)[:, None, None] * cotangent.astype(jnp.float32)
    d_out = weighted.astype(jnp.bfloat16).reshape(frames, rows, cols, width)
    flip_two = jnp.flip(conv_two, (0, 1, 2)).transpose(0, 1, 2, 4, 3)
    flip_one = jnp.flip(conv_one, (0, 1, 2)).transpose(0, 1, 2, 4, 3)
    d_h2 = correlate(jnp.pad(d_out, ((0, 2), (1, 1), (1, 1), (0, 0))), flip_two, frames, rows, cols)
    d_z1 = norm_back(z_one, gain_two, d_h2).astype(jnp.bfloat16)
    d_h1 = correlate(jnp.pad(d_z1, ((0, 2), (1, 1), (1, 1), (0, 0))), flip_one, frames, rows, cols)
    result = d_out.astype(jnp.float32) + norm_back(values, gain_one, d_h1)
    return result.astype(jnp.bfloat16).reshape(frames, rows, merged)
```

```python
import functools

import jax
import jax.numpy as jnp
from jax import lax
from jax.experimental import pallas as pl
from jax.experimental.pallas import tpu as pltpu
from jax.sharding import PartitionSpec as P

EPS = 1e-06
F32, BF16 = jnp.float32, jnp.bfloat16
VMEM_LIMIT = 48 * 1024 * 1024


def shifted(value, axis, steps):
    count = lax.axis_size(axis)
    first, last = (max(0, -steps), min(count, count - steps))
    return lax.ppermute(value, axis, [(source, source + steps) for source in range(first, last)])


def row_shifts(field):
    rows = field.shape[0]
    at = lax.broadcasted_iota(jnp.int32, field.shape, 0)
    above = jnp.where(at == 0, 0.0, pltpu.roll(field, 1, 0))
    below = jnp.where(at == rows - 1, 0.0, pltpu.roll(field, rows - 1, 0))
    return above.astype(BF16), field.astype(BF16), below.astype(BF16)


def lay_taps(dst, frame, column, field, columns):
    width = field.shape[1]
    for b, part in enumerate(row_shifts(field)):
        for e in range(3):
            if 0 <= column - e < columns:
                at = (b * 3 + e) * width
                dst[frame, column - e, :, at : at + width] = part


def turn_taps(dst, src):
    width = src.shape[-1]
    for a in range(3):
        for b in range(3):
            for e in range(3):
                at = (b * 3 + e) * width
                dst[a, :, at : at + width] = src[2 - a, 2 - b, 2 - e]


def conv(taps, kern, flipped):
    frames, columns, rows, depth = taps.shape
    size = (frames - 2) * columns * rows
    dims = (((1,), (1 if flipped else 0,)), ((), ()))
    total = None
    for a in range(3):
        left = taps[a : a + frames - 2].reshape(size, depth)
        right = kern[a] if flipped else kern[a].reshape(depth, kern.shape[-1])
        part = lax.dot_general(left, right, dims, preferred_element_type=F32)
        total = part if total is None else total + part
    return total


def scale_of(value):
    return lax.rsqrt(jnp.mean(value * value, axis=-1, keepdims=True) + EPS)


def norm_back(value, gain, grad):
    scale = scale_of(value)
    normed = value * scale
    act = normed * gain
    sig = 1.0 / (1.0 + jnp.exp(-act))
    d_norm = grad * sig * (1.0 + act * (1.0 - sig)) * gain
    return scale * (d_norm - normed * jnp.mean(d_norm * normed, axis=-1, keepdims=True))


def middle_kernel(edge, own, before, after, gain_one, gain_two, conv_one, conv_two, out, hid, grd, turned):
    width = gain_one.shape[-1]
    turn_taps(turned, conv_two)
    gain = gain_one[...]
    for frame in range(4):
        src, at = (before, frame) if frame < 2 else (own, frame - 2)
        for j in range(6):
            value = src[at, :, j * width : (j + 1) * width].astype(F32)
            act = value * scale_of(value) * gain
            lay_taps(hid, frame, j, act / (1.0 + jnp.exp(-act)), 4)
    for frame in range(4):
        src, at = (own, frame + 2) if frame < 2 else (after, frame - 2)
        for j in range(6):
            lay_taps(grd, frame, j, src[at, :, j * width : (j + 1) * width].astype(F32), 4)
    z_one = conv(hid, conv_one, False)
    d_h2 = conv(grd, turned, True)
    rows = own.shape[1]
    for frame in range(2):
        for c in range(4):
            part = slice((frame * 4 + c) * rows, (frame * 4 + c + 1) * rows)
            d_z = norm_back(z_one[part], gain_two[...], d_h2[part])
            if c in (0, 3):
                d_z = jnp.where(edge[c // 3] == 0, 0.0, d_z)
            out[frame, :, c * width : (c + 1) * width] = d_z.astype(BF16)


def last_kernel(own, d_own, d_after, gain_one, conv_one, out, grd, turned):
    width = gain_one.shape[-1]
    turn_taps(turned, conv_one)
    for frame in range(4):
        src, at = (d_own, frame) if frame < 2 else (d_after, frame - 2)
        for j in range(4):
            lay_taps(grd, frame, j, src[at, :, j * width : (j + 1) * width].astype(F32), 2)
    d_h1 = conv(grd, turned, True)
    rows = own.shape[1]
    for frame in range(2):
        for c in range(2):
            lanes = slice((c + 2) * width, (c + 3) * width)
            part = slice((frame * 2 + c) * rows, (frame * 2 + c + 1) * rows)
            value = own[frame, :, lanes].astype(F32)
            result = own[frame + 2, :, lanes].astype(F32) + norm_back(value, gain_one[...], d_h1[part])
            out[frame, :, c * width : (c + 1) * width] = result.astype(BF16)


def body(inputs, cotangent, frame_weight, gain_one, conv_one, gain_two, conv_two):
    tiles, me = lax.axis_size("tile"), lax.axis_index("tile")
    frames, _, merged = inputs.shape
    width = gain_one.shape[0]
    pair = merged // tiles
    params = pltpu.CompilerParams(vmem_limit_bytes=VMEM_LIMIT)
    vmem = pl.BlockSpec(memory_space=pltpu.VMEM)
    smem = pl.BlockSpec(memory_space=pltpu.SMEM)

    weighted = (frame_weight.astype(F32)[:, None, None] * cotangent.astype(F32)).astype(BF16)
    both = jnp.concatenate([inputs, weighted], axis=0).reshape(2 * frames, merged)
    both = jnp.pad(both, ((0, 0), (pair, pair)))
    blocks = jnp.stack([both[:, m * pair : (m + 3) * pair] for m in range(tiles)])
    held = lax.all_to_all(blocks, "tile", 0, 0)
    own = held.transpose(1, 0, 2)
    before = shifted(own[:frames], "tm", 1)
    after = shifted(own[frames:], "tm", -1)
    edge = jnp.stack([me > 0, me < tiles - 1]).astype(jnp.int32)
    gains = gain_one.reshape(1, width), gain_two.reshape(1, width)
    taps = 9 * width
    d_own = pl.pallas_call(
        middle_kernel,
        out_shape=jax.ShapeDtypeStruct((frames, tiles, 4 * width), BF16),
        in_specs=[smem] + [vmem] * 7,
        out_specs=vmem,
        scratch_shapes=[
            pltpu.VMEM((4, 4, tiles, taps), BF16),
            pltpu.VMEM((4, 4, tiles, taps), BF16),
            pltpu.VMEM((3, width, taps), BF16),
        ],
        compiler_params=params,
    )(edge, own, before, after, gains[0], gains[1], conv_one, conv_two)
    d_after = shifted(d_own, "tm", -1)
    return pl.pallas_call(
        last_kernel,
        out_shape=jax.ShapeDtypeStruct((frames, tiles, 2 * width), BF16),
        in_specs=[vmem] * 5,
        out_specs=vmem,
        scratch_shapes=[pltpu.VMEM((4, 2, tiles, taps), BF16), pltpu.VMEM((3, width, taps), BF16)],
        compiler_params=params,
    )(own, d_own, d_after, gains[0], conv_one)


def solution(mesh):
    in_specs = (P("tm", "tile", None), P("tm", "tile", None), P("tm"), P(), P(), P(), P())
    out_specs = P("tm", None, "tile")
    return jax.shard_map(body, mesh=mesh, in_specs=in_specs, out_specs=out_specs, check_vma=False)
```

```python
import jax
import jax.numpy as jnp
from jax import lax
from jax.experimental import pallas as pl
from jax.experimental.pallas import tpu as pltpu
from jax.sharding import Mesh
from jax.sharding import PartitionSpec as P

EPS = 1e-06
F32, BF16 = jnp.float32, jnp.bfloat16
MIB = 1024 * 1024


def shifted(value, axis, steps):
    count = lax.axis_size(axis)
    first, last = (max(0, -steps), min(count, count - steps))
    return lax.ppermute(value, axis, [(source, source + steps) for source in range(first, last)])


def spread(value):
    count = lax.axis_size("tm")
    later = [(2 * k, 2 * k + 2) for k in range(count - 1)]
    earlier = [(2 * k + 3, 2 * k + 1) for k in range(count - 1)]
    return lax.ppermute(value, ("tm", "core"), later + earlier)


def pack_kernel(weight, x, c, out, scale, x_here, dy, sems):
    tiles, frames, wide = out.shape
    pair = wide // 4
    moves = [
        pltpu.make_async_copy(src, dst, sems.at[n])
        for n, (src, dst) in enumerate(((weight, scale), (c, dy), (x, x_here)))
    ]
    for move in moves:
        move.start()
    none = jnp.zeros((frames, pair), BF16)
    for core in range(2):
        out[core, :, :pair] = none
        out[tiles - 2 + core, :, 3 * pair :] = none
    for move in moves[:2]:
        move.wait()
    at = lax.broadcasted_iota(jnp.int32, dy.shape, 0)
    factor = jnp.where(at == 0, scale[0].astype(F32), scale[1].astype(F32))
    dy[...] = (dy[...].astype(F32) * factor).astype(BF16)
    moves[2].wait()
    for q in range(tiles // 2):
        first, last = max(0, 2 * q - 1), min(tiles, 2 * q + 3)
        skip = first - (2 * q - 1)
        for core, src in ((0, x_here), (1, dy)):
            out[2 * q + core, :, skip * pair : (skip + last - first) * pair] = src[:, first * pair : last * pair]


def turn_kernel(conv_one, conv_two, one, two):
    width = conv_one.shape[-1]
    for src, dst in ((conv_two, two), (conv_one, one)):
        for a in range(3):
            for b in range(3):
                for e in range(3):
                    dst[a, b, :, e * width : (e + 1) * width] = src[2 - a, 2 - b, 2 - e]


def lefts(field, columns, width):
    odd = field[:, width:]
    parts = []
    for c in range(columns):
        src, at = (field, c) if c % 2 == 0 else (odd, c - 1)
        parts.append(src[:, at * width : (at + 3) * width])
    return jnp.concatenate(parts, axis=0)


def conv_sum(terms, kern, flipped, rows):
    dims = (((1,), (1 if flipped else 0,)), ((), ()))
    taps = []
    for b in range(3):
        total = None
        for a, left in terms:
            right = kern[a, b]
            if not flipped:
                right = right.reshape(left.shape[1], right.shape[-1])
            part = lax.dot_general(left, right, dims, preferred_element_type=F32)
            total = part if total is None else total + part
        taps.append(total)
    group = rows // 8
    at = lax.broadcasted_iota(jnp.int32, (group, taps[0].shape[1]), 0)
    blocks = []
    for first in range(0, taps[0].shape[0], rows):
        above, here, below = (tap[first : first + rows] for tap in taps)
        wrap = jnp.where(at == 0, 0.0, pltpu.roll(above[rows - group :], 1, 0))
        above = jnp.concatenate([wrap, above[: rows - group]], axis=0)
        wrap = jnp.where(at == group - 1, 0.0, pltpu.roll(below[:group], group - 1, 0))
        below = jnp.concatenate([below[group:], wrap], axis=0)
        blocks.append(here + above + below)
    return blocks


def scale_of(value):
    return lax.rsqrt(jnp.sum(value * value, axis=-1, keepdims=True) * (1.0 / value.shape[-1]) + EPS)


def sigmoid(value):
    return 0.5 * jnp.tanh(0.5 * value) + 0.5


def norm_back(value, gain, grad):
    scale = scale_of(value)
    normed = value * scale
    act = normed * gain
    sig = sigmoid(act)
    d_norm = grad * sig * (1.0 + act * (1.0 - sig)) * gain
    mean = jnp.sum(d_norm * normed, axis=-1, keepdims=True) * (1.0 / value.shape[-1])
    return scale * (d_norm - normed * mean)


def hidden(core, src, gain, hid):
    width = gain.shape[-1]
    rows = src.shape[2]
    first = lax.broadcasted_iota(jnp.int32, (rows, 2 * width), 1) < width
    gains = jnp.concatenate([gain, gain], axis=1)
    for frame in range(2):
        for p in range(3):
            lanes = pl.ds(pl.multiple_of((p + core) * 2 * width, 2 * width), 2 * width)
            value = src[0, frame, :, lanes].astype(F32)
            square = value * value
            left = jnp.sum(jnp.where(first, square, 0.0), axis=-1, keepdims=True)
            right = jnp.sum(jnp.where(first, 0.0, square), axis=-1, keepdims=True)
            left, right = (lax.rsqrt(part * (1.0 / width) + EPS) for part in (left, right))
            act = value * jnp.where(first, left, right) * gains
            hid[frame, :, p * 2 * width : (p + 1) * 2 * width] = (act * sigmoid(act)).astype(BF16)


def fields_of(core, src, gain, hid):
    width = gain.shape[-1]
    hidden(core, src, gain, hid)
    lanes = pl.ds(pl.multiple_of(core * 2 * width, 2 * width), 6 * width)
    return [lefts(hid[f], 4, width) for f in range(2)], [lefts(src[1, f, :, lanes], 4, width) for f in range(2)]


def own_kernel(place, own, gain_one, conv_one, turned, z_part, d_part, hid):
    rows = own.shape[2]
    xs, gs = fields_of(place[0], own, gain_one[...], hid)
    for t, terms in enumerate(([(2, xs[0])], [(1, xs[0]), (2, xs[1])])):
        for c, block in enumerate(conv_sum(terms, conv_one, False, rows)):
            z_part[t, c] = block
    for t, terms in enumerate(([(0, gs[0]), (1, gs[1])], [(0, gs[1])])):
        for c, block in enumerate(conv_sum(terms, turned, True, rows)):
            d_part[t, c] = block


def middle_kernel(
    place, other, z_part, d_part, two, gain_one, gain_two, conv_one, one, out, send, hid, z_all, d_all
):
    width = gain_one.shape[-1]
    rows = other.shape[2]
    xs, gs = fields_of(place[0], other, gain_one[...], hid)
    for t, terms in enumerate(([(0, xs[0]), (1, xs[1])], [(0, xs[1])])):
        for c, block in enumerate(conv_sum(terms, conv_one, False, rows)):
            z_all[t, c] = z_part[t, c] + block
    for t, terms in enumerate(([(2, gs[0])], [(1, gs[0]), (2, gs[1])])):
        for c, block in enumerate(conv_sum(terms, two, True, rows)):
            d_all[t, c] = d_part[t, c] + block
    for t in range(2):
        for c in range(4):
            d_z = norm_back(z_all[t, c], gain_two[...], d_all[t, c])
            if c in (0, 3):
                d_z = jnp.where(place[1 + c // 3] == 0, 0.0, d_z)
            out[t, :, c * width : (c + 1) * width] = d_z.astype(BF16)
    ds = [lefts(out[f], 2, width) for f in range(2)]
    for t, terms in enumerate(([(2, ds[0])], [(1, ds[0]), (2, ds[1])])):
        for c, block in enumerate(conv_sum(terms, one, True, rows)):
            send[t, :, c * width : (c + 1) * width] = block.astype(BF16)


def halves(first, value):
    left = jnp.sum(jnp.where(first, value, 0.0), axis=-1, keepdims=True)
    right = jnp.sum(jnp.where(first, 0.0, value), axis=-1, keepdims=True)
    return jnp.where(first, left, right)


def early_kernel(place, own, d_own, one, gain_one, base, slope, along, across, d_all):
    width = gain_one.shape[-1]
    rows = own.shape[2]
    ds = [lefts(d_own[f], 2, width) for f in range(2)]
    for t, terms in enumerate(([(0, ds[0]), (1, ds[1])], [(0, ds[1])])):
        for c, block in enumerate(conv_sum(terms, one, True, rows)):
            d_all[t, :, c * width : (c + 1) * width] = block
    lanes = pl.ds(pl.multiple_of((1 + place[0]) * 2 * width, 2 * width), 2 * width)
    first = lax.broadcasted_iota(jnp.int32, (rows, 2 * width), 1) < width
    gain = jnp.concatenate([gain_one[...]] * 2, axis=1)
    for t in range(2):
        value = own[0, t, :, lanes].astype(F32)
        scale = lax.rsqrt(halves(first, value * value) * (1.0 / width) + EPS)
        normed = value * scale
        act = normed * gain
        sig = sigmoid(act)
        turn = sig * (1.0 + act * (1.0 - sig)) * gain
        slope[t] = scale * turn
        along[t] = scale * normed * (1.0 / width)
        across[t] = turn * normed
        grad = d_all[t]
        total = halves(first, across[t] * grad)
        base[t] = own[1, t, :, lanes].astype(F32) + slope[t] * grad - along[t] * total


def last_kernel(late, base, slope, along, across, out, natural):
    rows = out.shape[1]
    group = rows // 8
    first = lax.broadcasted_iota(jnp.int32, late.shape[1:], 1) < late.shape[2] // 2
    for t in range(2):
        grad = late[t].astype(F32)
        result = base[t] + slope[t] * grad - along[t] * halves(first, across[t] * grad)
        for p in range(natural.shape[0]):
            for r in range(8):
                piece = result[r * group : (r + 1) * group, p * 128 : (p + 1) * 128]
                natural[p, pl.ds(r, group, stride=8), :] = piece
        for p in range(natural.shape[0]):
            out[t, :, p * 128 : (p + 1) * 128] = natural[p].astype(BF16)


def call(kernel, ins, outs, scratch, flops, *args, limit=16 * MIB):
    kinds = {"v": pltpu.VMEM, "s": pltpu.SMEM, "h": pltpu.HBM}
    return pl.pallas_call(
        kernel,
        out_shape=outs,
        in_specs=[pl.BlockSpec(memory_space=kinds[kind]) for kind in ins],
        out_specs=jax.tree.map(lambda _: pl.BlockSpec(memory_space=pltpu.VMEM), outs),
        scratch_shapes=scratch,
        compiler_params=pltpu.CompilerParams(vmem_limit_bytes=limit),
        cost_estimate=pl.CostEstimate(flops=flops, bytes_accessed=4 << 20, transcendentals=0),
    )(*args)


def body(inputs, cotangent, frame_weight, gain_one, conv_one, gain_two, conv_two):
    core = lax.axis_index("core")
    tiles, me = lax.axis_size(("chip", "core")), lax.axis_index(("chip", "core"))
    frames, _, merged = inputs.shape
    width = gain_one.shape[0]
    wide = 8 * width
    gain_one, gain_two = gain_one.reshape(1, width), gain_two.reshape(1, width)
    place = jnp.stack([core, me > 0, me < tiles - 1]).astype(jnp.int32)
    array = jax.ShapeDtypeStruct
    one = 2 * tiles * 9 * width * width

    local = [pltpu.SMEM((frames,), jnp.int32)] + [pltpu.VMEM((frames, merged), BF16)] * 2
    blocks = call(
        pack_kernel, "hhh", array((tiles, frames, wide), BF16), local + [pltpu.SemaphoreType.DMA((3,))], 10**6,
        frame_weight, inputs.reshape(frames, merged), cotangent.reshape(frames, merged), limit=60 * MIB,
    )
    held = lax.all_to_all(blocks, ("chip", "core"), 0, 0)
    held = held.reshape(tiles // 8, 8, frames, wide).transpose(2, 1, 0, 3).reshape(frames, tiles, wide)
    turned = array((3, 3, width, 3 * width), BF16)
    turned_one, turned_two = call(turn_kernel, "vv", (turned, turned), [], 10**9, conv_one, conv_two)
    held, turned_one, turned_two = lax.optimization_barrier((held, turned_one, turned_two))
    arrived = spread(held)
    own = lax.all_gather(held, "core")
    sums = (frames, 4, tiles, width)
    hid = pltpu.VMEM((frames, tiles, 6 * width), BF16)
    z_part, d_part = call(
        own_kernel, "svvvv", (array(sums, F32), array(sums, F32)), [hid], 24 * one,
        place, own, gain_one, conv_one, turned_two,
    )
    other = lax.all_gather(arrived, "core")
    d_own, send = call(
        middle_kernel, "svvvvvvvv",
        (array((frames, tiles, 4 * width), BF16), array((frames, tiles, 2 * width), BF16)),
        [hid, pltpu.VMEM(sums, F32), pltpu.VMEM(sums, F32)], 24 * one,
        place, other, z_part, d_part, turned_two, gain_one, gain_two, conv_one, turned_one,
    )
    late = shifted(send, "tm", -1)
    field = (frames, tiles, 2 * width)
    parts = call(
        early_kernel, "svvvv", (array(field, F32),) * 4, [pltpu.VMEM(field, F32)], 6 * one,
        place, own, d_own, turned_one, gain_one,
    )
    natural = pltpu.VMEM((2 * width // 128, tiles, 128), F32)
    return call(last_kernel, "vvvvv", array(field, BF16), [natural], one, late, *parts)


def solution(mesh):
    tm, tile = mesh.devices.shape
    chips = Mesh(mesh.devices.reshape(tm, tile // 2, 2), ("tm", "chip", "core"))
    tiles = ("chip", "core")
    in_specs = (P("tm", tiles, None), P("tm", tiles, None), P("tm"), P(), P(), P(), P())
    out_specs = P("tm", None, tiles)
    return jax.shard_map(body, mesh=chips, in_specs=in_specs, out_specs=out_specs, check_vma=False)
```

```python
import jax
import jax.numpy as jnp
from jax import lax
from jax.experimental import pallas as pl
from jax.experimental.pallas import tpu as pltpu
from jax.sharding import Mesh
from jax.sharding import PartitionSpec as P

EPS = 1e-06
F32, BF16 = jnp.float32, jnp.bfloat16
MIB = 1024 * 1024


def shifted(value, axis, steps):
    count = lax.axis_size(axis)
    first, last = (max(0, -steps), min(count, count - steps))
    return lax.ppermute(value, axis, [(source, source + steps) for source in range(first, last)])


def spread(value):
    count = lax.axis_size("tm")
    later = [(2 * k, 2 * k + 2) for k in range(count - 1)]
    earlier = [(2 * k + 3, 2 * k + 1) for k in range(count - 1)]
    return lax.ppermute(value, ("tm", "core"), later + earlier)


def pack_kernel(weight, x, c, out, scale, x_here, dy, x_blocks, dy_blocks, sems):
    chips, _, frames, wide = out.shape
    pair = wide // 4
    moves = [
        pltpu.make_async_copy(src, dst, sems.at[n])
        for n, (src, dst) in enumerate(((x, x_here), (c, dy), (weight, scale)))
    ]
    for move in moves:
        move.start()

    def lay(src, blocks, kind):
        none = jnp.zeros((frames, pair), BF16)
        blocks[0, :, :pair] = none
        blocks[chips - 1, :, 3 * pair :] = none
        for q in range(chips):
            first, last = max(0, 2 * q - 1), min(2 * chips, 2 * q + 3)
            skip = first - (2 * q - 1)
            blocks[q, :, skip * pair : (skip + last - first) * pair] = src[:, first * pair : last * pair]
        move = pltpu.make_async_copy(blocks, out.at[:, kind], sems.at[3 + kind])
        move.start()
        return move

    moves[0].wait()
    x_move = lay(x_here, x_blocks, 0)
    moves[1].wait()
    moves[2].wait()
    at = lax.broadcasted_iota(jnp.int32, dy.shape, 0)
    factor = jnp.where(at == 0, scale[0].astype(F32), scale[1].astype(F32)).astype(BF16)
    dy[...] = dy[...] * factor
    dy_move = lay(dy, dy_blocks, 1)
    x_move.wait()
    dy_move.wait()


def turn_kernel(conv_one, conv_two, one, two):
    width = conv_one.shape[-1]
    for src, dst in ((conv_two, two), (conv_one, one)):
        for a in range(3):
            for b in range(3):
                for e in range(3):
                    dst[a, b, :, e * width : (e + 1) * width] = src[2 - a, 2 - b, 2 - e]


def lefts(field, columns, width):
    odd = field[:, width:]
    parts = []
    for c in range(columns):
        src, at = (field, c) if c % 2 == 0 else (odd, c - 1)
        parts.append(src[:, at * width : (at + 3) * width])
    return jnp.concatenate(parts, axis=0)


def conv_sum(terms, kern, flipped, rows):
    dims = (((1,), (1 if flipped else 0,)), ((), ()))
    taps = []
    for b in range(3):
        total = None
        for a, left in terms:
            right = kern[a, b]
            if not flipped:
                right = right.reshape(left.shape[1], right.shape[-1])
            part = lax.dot_general(left, right, dims, preferred_element_type=F32)
            total = part if total is None else total + part
        taps.append(total)
    group = rows // 8
    at = lax.broadcasted_iota(jnp.int32, (group, taps[0].shape[1]), 0)
    blocks = []
    for first in range(0, taps[0].shape[0], rows):
        above, here, below = (tap[first : first + rows] for tap in taps)
        wrap = jnp.where(at == 0, 0.0, pltpu.roll(above[rows - group :], 1, 0))
        above = jnp.concatenate([wrap, above[: rows - group]], axis=0)
        wrap = jnp.where(at == group - 1, 0.0, pltpu.roll(below[:group], group - 1, 0))
        below = jnp.concatenate([below[group:], wrap], axis=0)
        blocks.append(here + above + below)
    return blocks


def scale_of(value):
    return lax.rsqrt(jnp.sum(value * value, axis=-1, keepdims=True) * (1.0 / value.shape[-1]) + EPS)


def norm_back(value, gain, grad):
    scale = scale_of(value)
    normed = value * scale
    half = 0.5 * gain
    h = normed * half
    t = jnp.tanh(h)
    d_norm = grad * ((1.0 + t) * (1.0 + h - h * t)) * half
    mean = jnp.sum(d_norm * normed, axis=-1, keepdims=True) * (1.0 / value.shape[-1])
    return scale * (d_norm - normed * mean)


def thirds(value):
    part = value.shape[-1] // 3
    return [value[:, p * part : (p + 1) * part] for p in range(3)]


def two_sums(value):
    left, middle, right = thirds(value)
    first = lax.broadcasted_iota(jnp.int32, middle.shape, 1) < middle.shape[1] // 2
    left = jnp.sum(left + jnp.where(first, middle, 0.0), axis=-1, keepdims=True)
    right = jnp.sum(right + jnp.where(first, 0.0, middle), axis=-1, keepdims=True)
    return left, right, first


def hidden(core, src, gain, hid):
    width = gain.shape[-1]
    part = 2 * width // 3
    gains = thirds(jnp.concatenate([gain, gain], axis=1))
    for frame in range(2):
        for p in range(3):
            lanes = pl.ds(pl.multiple_of((p + core) * 2 * width, 2 * width), 2 * width)
            value = src[0, frame, :, lanes].astype(F32)
            left, right, first = two_sums(value * value)
            left, right = (0.5 * lax.rsqrt(total * (1.0 / width) + EPS) for total in (left, right))
            scales = left, jnp.where(first, left, right), right
            for n, (piece, scale, g) in enumerate(zip(thirds(value), scales, gains)):
                h = piece * scale * g
                at = p * 2 * width + n * part
                hid[frame, :, at : at + part] = (h + h * jnp.tanh(h)).astype(BF16)


def fields_of(core, src, gain, hid):
    width = gain.shape[-1]
    hidden(core, src, gain, hid)
    lanes = pl.ds(pl.multiple_of(core * 2 * width, 2 * width), 6 * width)
    return [lefts(hid[f], 4, width) for f in range(2)], [lefts(src[1, f, :, lanes], 4, width) for f in range(2)]


def own_kernel(own, gain_one, conv_one, turned, z_part, d_part, hid):
    rows = own.shape[2]
    xs, gs = fields_of(lax.axis_index("core"), own, gain_one[...], hid)
    for t, terms in enumerate(([(2, xs[0])], [(1, xs[0]), (2, xs[1])])):
        for c, block in enumerate(conv_sum(terms, conv_one, False, rows)):
            z_part[t, c] = block
    for t, terms in enumerate(([(0, gs[0]), (1, gs[1])], [(0, gs[1])])):
        for c, block in enumerate(conv_sum(terms, turned, True, rows)):
            d_part[t, c] = block


def middle_kernel(
    other, z_part, d_part, two, gain_one, gain_two, conv_one, one, out, send, hid, z_all, d_all
):
    width = gain_one.shape[-1]
    rows = other.shape[2]
    xs, gs = fields_of(lax.axis_index("core"), other, gain_one[...], hid)
    for t, terms in enumerate(([(0, xs[0]), (1, xs[1])], [(0, xs[1])])):
        for c, block in enumerate(conv_sum(terms, conv_one, False, rows)):
            z_all[t, c] = z_part[t, c] + block
    for t, terms in enumerate(([(2, gs[0])], [(1, gs[0]), (2, gs[1])])):
        for c, block in enumerate(conv_sum(terms, two, True, rows)):
            d_all[t, c] = d_part[t, c] + block
    me, last = lax.axis_index(("chip", "core")), lax.axis_size(("chip", "core")) - 1
    outside = {0: me == 0, 3: me == last}

    def back(t):
        for c in range(4):
            d_z = norm_back(z_all[t, c], gain_two[...], d_all[t, c])
            if c in outside:
                d_z = jnp.where(outside[c], 0.0, d_z)
            out[t, :, c * width : (c + 1) * width] = d_z.astype(BF16)
        return lefts(out[t], 2, width)

    def give(t, blocks):
        for c, block in enumerate(blocks):
            send[t, :, c * width : (c + 1) * width] = block.astype(BF16)

    d_first = back(0)
    give(0, conv_sum([(2, d_first)], one, True, rows))
    middle = conv_sum([(1, d_first)], one, True, rows)
    late = conv_sum([(2, back(1))], one, True, rows)
    give(1, [a + b for a, b in zip(middle, late)])


def halves(value):
    left, right, first = two_sums(value)
    shape = first.shape
    pieces = jnp.broadcast_to(left, shape), jnp.where(first, left, right), jnp.broadcast_to(right, shape)
    return jnp.concatenate(pieces, axis=1)


def early_kernel(own, d_own, one, gain_one, base, slope, along, across, d_all):
    width = gain_one.shape[-1]
    rows = own.shape[2]
    ds = [lefts(d_own[f], 2, width) for f in range(2)]
    for t, terms in enumerate(([(0, ds[0]), (1, ds[1])], [(0, ds[1])])):
        for c, block in enumerate(conv_sum(terms, one, True, rows)):
            d_all[t, :, c * width : (c + 1) * width] = block
    lanes = pl.ds(pl.multiple_of((1 + lax.axis_index("core")) * 2 * width, 2 * width), 2 * width)
    gain = jnp.concatenate([gain_one[...]] * 2, axis=1)
    for t in range(2):
        value = own[0, t, :, lanes].astype(F32)
        scale = lax.rsqrt(halves(value * value) * (1.0 / width) + EPS)
        normed = value * scale
        h = normed * (0.5 * gain)
        bend = jnp.tanh(h)
        turn = (1.0 + bend) * (1.0 + h - h * bend) * (0.5 * gain)
        slope[t] = scale * turn
        along[t] = scale * normed * (1.0 / width)
        across[t] = turn * normed
        grad = d_all[t]
        total = halves(across[t] * grad)
        base[t] = own[1, t, :, lanes].astype(F32) + slope[t] * grad - along[t] * total


def last_kernel(late, base, slope, along, across, out, natural):
    rows = out.shape[1]
    group = rows // 8
    for t in range(2):
        grad = late[t].astype(F32)
        result = base[t] + slope[t] * grad - along[t] * halves(across[t] * grad)
        for p in range(natural.shape[0]):
            for r in range(8):
                piece = result[r * group : (r + 1) * group, p * 128 : (p + 1) * 128]
                natural[p, pl.ds(r, group, stride=8), :] = piece
        for p in range(natural.shape[0]):
            out[t, :, p * 128 : (p + 1) * 128] = natural[p].astype(BF16)


def call(kernel, ins, outs, scratch, flops, *args, limit=16 * MIB, to="v"):
    kinds = {"v": pltpu.VMEM, "s": pltpu.SMEM, "h": pltpu.HBM}
    return pl.pallas_call(
        kernel,
        out_shape=outs,
        in_specs=[pl.BlockSpec(memory_space=kinds[kind]) for kind in ins],
        out_specs=jax.tree.map(lambda _: pl.BlockSpec(memory_space=kinds[to]), outs),
        scratch_shapes=scratch,
        compiler_params=pltpu.CompilerParams(vmem_limit_bytes=limit),
        cost_estimate=pl.CostEstimate(flops=flops, bytes_accessed=4 << 20, transcendentals=0),
    )(*args)


def body(inputs, cotangent, frame_weight, gain_one, conv_one, gain_two, conv_two):
    tiles = lax.axis_size(("chip", "core"))
    frames, _, merged = inputs.shape
    width = gain_one.shape[0]
    wide = 8 * width
    gain_one, gain_two = gain_one.reshape(1, width), gain_two.reshape(1, width)
    array = jax.ShapeDtypeStruct
    one = 2 * tiles * 9 * width * width

    local = [pltpu.SMEM((frames,), jnp.int32)] + [pltpu.VMEM((frames, merged), BF16)] * 2
    local += [pltpu.VMEM((tiles // 2, frames, wide), BF16)] * 2
    blocks = call(
        pack_kernel, "hhh", array((tiles // 2, 2, frames, wide), BF16), local + [pltpu.SemaphoreType.DMA((5,))], 10**6,
        frame_weight, inputs.reshape(frames, merged), cotangent.reshape(frames, merged), limit=60 * MIB, to="h",
    ).reshape(tiles, frames, wide)
    held = lax.all_to_all(blocks, ("chip", "core"), 0, 0)
    held = held.reshape(tiles // 8, 8, frames, wide).transpose(2, 1, 0, 3).reshape(frames, tiles, wide)
    turned = array((3, 3, width, 3 * width), BF16)
    turned_one, turned_two = call(turn_kernel, "vv", (turned, turned), [], 10**9, conv_one, conv_two)
    held, turned_one, turned_two = lax.optimization_barrier((held, turned_one, turned_two))
    arrived = spread(held)
    own = lax.all_gather(held, "core")
    sums = (frames, 4, tiles, width)
    hid = pltpu.VMEM((frames, tiles, 6 * width), BF16)
    z_part, d_part = call(
        own_kernel, "vvvv", (array(sums, F32), array(sums, F32)), [hid], 24 * one,
        own, gain_one, conv_one, turned_two,
    )
    other = lax.all_gather(arrived, "core")
    d_own, send = call(
        middle_kernel, "vvvvvvvv",
        (array((frames, tiles, 4 * width), BF16), array((frames, tiles, 2 * width), BF16)),
        [hid, pltpu.VMEM(sums, F32), pltpu.VMEM(sums, F32)], 24 * one,
        other, z_part, d_part, turned_two, gain_one, gain_two, conv_one, turned_one,
    )
    late = shifted(send, "tm", -1)
    field = (frames, tiles, 2 * width)
    parts = call(
        early_kernel, "vvvv", (array(field, F32),) * 4, [pltpu.VMEM(field, F32)], 6 * one,
        own, d_own, turned_one, gain_one,
    )
    natural = pltpu.VMEM((2 * width // 128, tiles, 128), F32)
    return call(last_kernel, "vvvvv", array(field, BF16), [natural], one, late, *parts)


def solution(mesh):
    tm, tile = mesh.devices.shape
    chips = Mesh(mesh.devices.reshape(tm, tile // 2, 2), ("tm", "chip", "core"))
    tiles = ("chip", "core")
    in_specs = (P("tm", tiles, None), P("tm", tiles, None), P("tm"), P(), P(), P(), P())
    out_specs = P("tm", None, tiles)
    return jax.shard_map(body, mesh=chips, in_specs=in_specs, out_specs=out_specs, check_vma=False)
```

```python
import jax
import jax.numpy as jnp
from jax import lax
from jax.experimental import pallas as pl
from jax.experimental.pallas import tpu as pltpu
from jax.sharding import Mesh
from jax.sharding import PartitionSpec as P

EPS = 1e-06
F32, BF16 = jnp.float32, jnp.bfloat16
MIB = 1024 * 1024


def shifted(value, axis, steps):
    count = lax.axis_size(axis)
    first, last = (max(0, -steps), min(count, count - steps))
    return lax.ppermute(value, axis, [(source, source + steps) for source in range(first, last)])


def x_core(block, count):
    return jnp.where(block == count // 2 - 1, 1, 0)


def x_core_other(block, count):
    return jnp.where(block == count // 2, 1, 0)


def spread(value):
    count = lax.axis_size("tm")
    here = [1 if k == count // 2 - 1 else 0 for k in range(count)]
    there = [1 if k == count // 2 else 0 for k in range(count)]
    later = [(2 * k + here[k], 2 * k + 2 + there[k + 1]) for k in range(count - 1)]
    earlier = [(2 * k + 3 - here[k + 1], 2 * k + 1 - there[k]) for k in range(count - 1)]
    return lax.ppermute(value, ("tm", "core"), later + earlier)


def pack_kernel(weight, x, c, out, scale, x_here, dy, x_blocks, dy_blocks, sems):
    chips, _, frames, wide = out.shape
    pair = wide // 4
    moves = [
        pltpu.make_async_copy(src, dst, sems.at[n])
        for n, (src, dst) in enumerate(((x, x_here), (c, dy), (weight, scale)))
    ]
    for move in moves:
        move.start()

    def lay(src, blocks, core, kind):
        none = jnp.zeros((frames, pair), BF16)
        blocks[0, :, :pair] = none
        blocks[chips - 1, :, 3 * pair :] = none
        for q in range(chips):
            first, last = max(0, 2 * q - 1), min(2 * chips, 2 * q + 3)
            skip = first - (2 * q - 1)
            blocks[q, :, skip * pair : (skip + last - first) * pair] = src[:, first * pair : last * pair]
        move = pltpu.make_async_copy(blocks, out.at[:, core], sems.at[3 + kind])
        move.start()
        return move

    first = x_core(lax.axis_index("tm"), lax.axis_size("tm"))
    moves[0].wait()
    x_move = lay(x_here, x_blocks, first, 0)
    moves[1].wait()
    moves[2].wait()
    at = lax.broadcasted_iota(jnp.int32, dy.shape, 0)
    factor = jnp.where(at == 0, scale[0].astype(F32), scale[1].astype(F32)).astype(BF16)
    dy[...] = dy[...] * factor
    dy_move = lay(dy, dy_blocks, 1 - first, 1)
    x_move.wait()
    dy_move.wait()


def turn_kernel(src, dst):
    width = src.shape[-1]
    for a in range(3):
        for b in range(3):
            for e in range(3):
                dst[a, b, :, e * width : (e + 1) * width] = src[2 - a, 2 - b, 2 - e]


def lefts(field, columns, width):
    odd = field[:, width:]
    parts = []
    for c in range(columns):
        src, at = (field, c) if c % 2 == 0 else (odd, c - 1)
        parts.append(src[:, at * width : (at + 3) * width])
    return jnp.concatenate(parts, axis=0)


def conv_sum(terms, kern, flipped, rows):
    dims = (((1,), (1 if flipped else 0,)), ((), ()))
    taps = []
    for b in range(3):
        total = None
        for a, left in terms:
            right = kern[a, b]
            if not flipped:
                right = right.reshape(left.shape[1], right.shape[-1])
            part = lax.dot_general(left, right, dims, preferred_element_type=F32)
            total = part if total is None else total + part
        taps.append(total)
    group = rows // 8
    at = lax.broadcasted_iota(jnp.int32, (group, taps[0].shape[1]), 0)
    blocks = []
    for first in range(0, taps[0].shape[0], rows):
        above, here, below = (tap[first : first + rows] for tap in taps)
        wrap = jnp.where(at == 0, 0.0, pltpu.roll(above[rows - group :], 1, 0))
        above = jnp.concatenate([wrap, above[: rows - group]], axis=0)
        wrap = jnp.where(at == group - 1, 0.0, pltpu.roll(below[:group], group - 1, 0))
        below = jnp.concatenate([below[group:], wrap], axis=0)
        blocks.append(here + above + below)
    return blocks


def scale_of(value):
    return lax.rsqrt(jnp.sum(value * value, axis=-1, keepdims=True) * (1.0 / value.shape[-1]) + EPS)


def norm_back(value, gain, grad):
    scale = scale_of(value)
    normed = value * scale
    half = 0.5 * gain
    h = normed * half
    t = jnp.tanh(h)
    d_norm = grad * ((1.0 + t) * (1.0 + h - h * t)) * half
    mean = jnp.sum(d_norm * normed, axis=-1, keepdims=True) * (1.0 / value.shape[-1])
    return scale * (d_norm - normed * mean)


def thirds(value):
    part = value.shape[-1] // 3
    return [value[:, p * part : (p + 1) * part] for p in range(3)]


def two_sums(value):
    left, middle, right = thirds(value)
    first = lax.broadcasted_iota(jnp.int32, middle.shape, 1) < middle.shape[1] // 2
    left = jnp.sum(left + jnp.where(first, middle, 0.0), axis=-1, keepdims=True)
    right = jnp.sum(right + jnp.where(first, 0.0, middle), axis=-1, keepdims=True)
    return left, right, first


def hidden(core, kind, src, gain, hid):
    width = gain.shape[-1]
    part = 2 * width // 3
    gains = thirds(jnp.concatenate([gain, gain], axis=1))
    for frame in range(2):
        for p in range(3):
            lanes = pl.ds(pl.multiple_of((p + core) * 2 * width, 2 * width), 2 * width)
            value = src[kind, frame, :, lanes].astype(F32)
            left, right, first = two_sums(value * value)
            left, right = (0.5 * lax.rsqrt(total * (1.0 / width) + EPS) for total in (left, right))
            scales = left, jnp.where(first, left, right), right
            for n, (piece, scale, g) in enumerate(zip(thirds(value), scales, gains)):
                h = piece * scale * g
                at = p * 2 * width + n * part
                hid[frame, :, at : at + part] = (h + h * jnp.tanh(h)).astype(BF16)


def fields_of(core, kind, src, gain, hid):
    width = gain.shape[-1]
    hidden(core, kind, src, gain, hid)
    lanes = pl.ds(pl.multiple_of(core * 2 * width, 2 * width), 6 * width)
    return [lefts(hid[f], 4, width) for f in range(2)], [lefts(src[1 - kind, f, :, lanes], 4, width) for f in range(2)]


def own_kernel(own, gain_one, conv_one, turned, z_part, d_part, hid):
    rows = own.shape[2]
    xs, gs = fields_of(lax.axis_index("core"), x_core(lax.axis_index("tm"), lax.axis_size("tm")), own, gain_one[...], hid)
    for t, terms in enumerate(([(2, xs[0])], [(1, xs[0]), (2, xs[1])])):
        for c, block in enumerate(conv_sum(terms, conv_one, False, rows)):
            z_part[t, c] = block
    for t, terms in enumerate(([(0, gs[0]), (1, gs[1])], [(0, gs[1])])):
        for c, block in enumerate(conv_sum(terms, turned, True, rows)):
            d_part[t, c] = block


def middle_kernel(
    other, z_part, d_part, two, gain_one, gain_two, conv_one, one, out, send, hid, z_all, d_all
):
    width = gain_one.shape[-1]
    rows = other.shape[2]
    xs, gs = fields_of(lax.axis_index("core"), x_core_other(lax.axis_index("tm"), lax.axis_size("tm")), other, gain_one[...], hid)
    for t, terms in enumerate(([(0, xs[0]), (1, xs[1])], [(0, xs[1])])):
        for c, block in enumerate(conv_sum(terms, conv_one, False, rows)):
            z_all[t, c] = z_part[t, c] + block
    for t, terms in enumerate(([(2, gs[0])], [(1, gs[0]), (2, gs[1])])):
        for c, block in enumerate(conv_sum(terms, two, True, rows)):
            d_all[t, c] = d_part[t, c] + block
    me, last = lax.axis_index(("chip", "core")), lax.axis_size(("chip", "core")) - 1
    outside = {0: me == 0, 3: me == last}

    def back(t):
        for c in range(4):
            d_z = norm_back(z_all[t, c], gain_two[...], d_all[t, c])
            if c in outside:
                d_z = jnp.where(outside[c], 0.0, d_z)
            out[t, :, c * width : (c + 1) * width] = d_z.astype(BF16)
        return lefts(out[t], 2, width)

    def give(t, blocks):
        for c, block in enumerate(blocks):
            send[t, :, c * width : (c + 1) * width] = block.astype(BF16)

    d_first = back(0)
    give(0, conv_sum([(2, d_first)], one, True, rows))
    middle = conv_sum([(1, d_first)], one, True, rows)
    late = conv_sum([(2, back(1))], one, True, rows)
    give(1, [a + b for a, b in zip(middle, late)])


def halves(value):
    left, right, first = two_sums(value)
    shape = first.shape
    pieces = jnp.broadcast_to(left, shape), jnp.where(first, left, right), jnp.broadcast_to(right, shape)
    return jnp.concatenate(pieces, axis=1)


def early_kernel(own, d_own, one, gain_one, base, slope, along, across, d_all):
    width = gain_one.shape[-1]
    rows = own.shape[2]
    ds = [lefts(d_own[f], 2, width) for f in range(2)]
    for t, terms in enumerate(([(0, ds[0]), (1, ds[1])], [(0, ds[1])])):
        for c, block in enumerate(conv_sum(terms, one, True, rows)):
            d_all[t, :, c * width : (c + 1) * width] = block
    lanes = pl.ds(pl.multiple_of((1 + lax.axis_index("core")) * 2 * width, 2 * width), 2 * width)
    gain = jnp.concatenate([gain_one[...]] * 2, axis=1)
    kind = x_core(lax.axis_index("tm"), lax.axis_size("tm"))
    for t in range(2):
        value = own[kind, t, :, lanes].astype(F32)
        scale = lax.rsqrt(halves(value * value) * (1.0 / width) + EPS)
        normed = value * scale
        h = normed * (0.5 * gain)
        bend = jnp.tanh(h)
        turn = (1.0 + bend) * (1.0 + h - h * bend) * (0.5 * gain)
        slope[t] = scale * turn
        along[t] = scale * normed * (1.0 / width)
        across[t] = turn * normed
        grad = d_all[t]
        total = halves(across[t] * grad)
        base[t] = own[1 - kind, t, :, lanes].astype(F32) + slope[t] * grad - along[t] * total


def last_kernel(late, base, slope, along, across, out, natural):
    rows = out.shape[1]
    group = rows // 8
    for t in range(2):
        grad = late[t].astype(F32)
        result = base[t] + slope[t] * grad - along[t] * halves(across[t] * grad)
        for p in range(natural.shape[0]):
            for r in range(8):
                piece = result[r * group : (r + 1) * group, p * 128 : (p + 1) * 128]
                natural[p, pl.ds(r, group, stride=8), :] = piece
        for p in range(natural.shape[0]):
            out[t, :, p * 128 : (p + 1) * 128] = natural[p].astype(BF16)


def call(kernel, ins, outs, scratch, flops, *args, limit=16 * MIB, to="v"):
    kinds = {"v": pltpu.VMEM, "s": pltpu.SMEM, "h": pltpu.HBM}
    return pl.pallas_call(
        kernel,
        out_shape=outs,
        in_specs=[pl.BlockSpec(memory_space=kinds[kind]) for kind in ins],
        out_specs=jax.tree.map(lambda _: pl.BlockSpec(memory_space=kinds[to]), outs),
        scratch_shapes=scratch,
        compiler_params=pltpu.CompilerParams(vmem_limit_bytes=limit),
        cost_estimate=pl.CostEstimate(flops=flops, bytes_accessed=4 << 20, transcendentals=0),
    )(*args)


def body(inputs, cotangent, frame_weight, gain_one, conv_one, gain_two, conv_two):
    tiles = lax.axis_size(("chip", "core"))
    frames, _, merged = inputs.shape
    width = gain_one.shape[0]
    wide = 8 * width
    gain_one, gain_two = gain_one.reshape(1, width), gain_two.reshape(1, width)
    array = jax.ShapeDtypeStruct
    one = 2 * tiles * 9 * width * width

    local = [pltpu.SMEM((frames,), jnp.int32)] + [pltpu.VMEM((frames, merged), BF16)] * 2
    local += [pltpu.VMEM((tiles // 2, frames, wide), BF16)] * 2
    blocks = call(
        pack_kernel, "hhh", array((tiles // 2, 2, frames, wide), BF16), local + [pltpu.SemaphoreType.DMA((5,))], 10**6,
        frame_weight, inputs.reshape(frames, merged), cotangent.reshape(frames, merged), limit=60 * MIB, to="h",
    ).reshape(tiles, frames, wide)
    held = lax.all_to_all(blocks, ("chip", "core"), 0, 0)
    held = held.reshape(tiles // 8, 8, frames, wide).transpose(2, 1, 0, 3).reshape(frames, tiles, wide)
    turned = array((3, 3, width, 3 * width), BF16)
    turned_two = call(turn_kernel, "v", turned, [], 10**9, conv_two)
    held, turned_two = lax.optimization_barrier((held, turned_two))
    arrived = spread(held)
    own = lax.all_gather(held, "core")
    turned_one = call(turn_kernel, "v", turned, [], 10**9, conv_one)
    sums = (frames, 4, tiles, width)
    hid = pltpu.VMEM((frames, tiles, 6 * width), BF16)
    z_part, d_part = call(
        own_kernel, "vvvv", (array(sums, F32), array(sums, F32)), [hid], 24 * one,
        own, gain_one, conv_one, turned_two,
    )
    other = lax.all_gather(arrived, "core")
    d_own, send = call(
        middle_kernel, "vvvvvvvv",
        (array((frames, tiles, 4 * width), BF16), array((frames, tiles, 2 * width), BF16)),
        [hid, pltpu.VMEM(sums, F32), pltpu.VMEM(sums, F32)], 24 * one,
        other, z_part, d_part, turned_two, gain_one, gain_two, conv_one, turned_one,
    )
    late = shifted(send, "tm", -1)
    field = (frames, tiles, 2 * width)
    parts = call(
        early_kernel, "vvvv", (array(field, F32),) * 4, [pltpu.VMEM(field, F32)], 6 * one,
        own, d_own, turned_one, gain_one,
    )
    natural = pltpu.VMEM((2 * width // 128, tiles, 128), F32)
    return call(last_kernel, "vvvvv", array(field, BF16), [natural], one, late, *parts)


def solution(mesh):
    tm, tile = mesh.devices.shape
    chips = Mesh(mesh.devices.reshape(tm, tile // 2, 2), ("tm", "chip", "core"))
    tiles = ("chip", "core")
    in_specs = (P("tm", tiles, None), P("tm", tiles, None), P("tm"), P(), P(), P(), P())
    out_specs = P("tm", None, tiles)
    return jax.shard_map(body, mesh=chips, in_specs=in_specs, out_specs=out_specs, check_vma=False)
```

```python
import jax
import jax.numpy as jnp
from jax import lax
from jax.experimental import pallas as pl
from jax.experimental.pallas import tpu as pltpu
from jax.sharding import Mesh
from jax.sharding import PartitionSpec as P

EPS = 1e-06
F32, BF16 = jnp.float32, jnp.bfloat16
MIB = 1024 * 1024


def shifted(value, axis, steps):
    count = lax.axis_size(axis)
    first, last = (max(0, -steps), min(count, count - steps))
    return lax.ppermute(value, axis, [(source, source + steps) for source in range(first, last)])


def x_core(block, count):
    return jnp.where(block == count // 2 - 1, 1, 0)


def x_core_other(block, count):
    return jnp.where(block == count // 2, 1, 0)


def spread(value):
    count = lax.axis_size("tm")
    here = [1 if k == count // 2 - 1 else 0 for k in range(count)]
    there = [1 if k == count // 2 else 0 for k in range(count)]
    later = [(2 * k + here[k], 2 * k + 2 + there[k + 1]) for k in range(count - 1)]
    earlier = [(2 * k + 3 - here[k + 1], 2 * k + 1 - there[k]) for k in range(count - 1)]
    return lax.ppermute(value, ("tm", "core"), later + earlier)


def pack_kernel(weight, x, c, out, scale, x_here, dy, x_blocks, dy_blocks, sems):
    chips, _, frames, wide = out.shape
    pair = wide // 4
    moves = [
        pltpu.make_async_copy(src, dst, sems.at[n])
        for n, (src, dst) in enumerate(((x, x_here), (c, dy), (weight, scale)))
    ]
    for move in moves:
        move.start()

    def lay(src, blocks, core, kind):
        none = jnp.zeros((frames, pair), BF16)
        blocks[0, :, :pair] = none
        blocks[chips - 1, :, 3 * pair :] = none
        for q in range(chips):
            first, last = max(0, 2 * q - 1), min(2 * chips, 2 * q + 3)
            skip = first - (2 * q - 1)
            blocks[q, :, skip * pair : (skip + last - first) * pair] = src[:, first * pair : last * pair]
        move = pltpu.make_async_copy(blocks, out.at[:, core], sems.at[3 + kind])
        move.start()
        return move

    first = x_core(lax.axis_index("tm"), lax.axis_size("tm"))
    moves[0].wait()
    x_move = lay(x_here, x_blocks, first, 0)
    moves[1].wait()
    moves[2].wait()
    at = lax.broadcasted_iota(jnp.int32, dy.shape, 0)
    factor = jnp.where(at == 0, scale[0].astype(F32), scale[1].astype(F32)).astype(BF16)
    dy[...] = dy[...] * factor
    dy_move = lay(dy, dy_blocks, 1 - first, 1)
    x_move.wait()
    dy_move.wait()


def turn_kernel(src, dst):
    width = src.shape[-1]
    for a in range(3):
        for b in range(3):
            for e in range(3):
                dst[a, b, :, e * width : (e + 1) * width] = src[2 - a, 2 - b, 2 - e]


def lefts(field, columns, width):
    odd = field[:, width:]
    parts = []
    for c in range(columns):
        src, at = (field, c) if c % 2 == 0 else (odd, c - 1)
        parts.append(src[:, at * width : (at + 3) * width])
    return jnp.concatenate(parts, axis=0)


def conv_sum(terms, kern, flipped, rows):
    dims = (((1,), (1 if flipped else 0,)), ((), ()))
    taps = []
    for b in range(3):
        total = None
        for a, left in terms:
            right = kern[a, b]
            if not flipped:
                right = right.reshape(left.shape[1], right.shape[-1])
            part = lax.dot_general(left, right, dims, preferred_element_type=F32)
            total = part if total is None else total + part
        taps.append(total)
    group = rows // 8
    at = lax.broadcasted_iota(jnp.int32, (group, taps[0].shape[1]), 0)
    blocks = []
    for first in range(0, taps[0].shape[0], rows):
        above, here, below = (tap[first : first + rows] for tap in taps)
        wrap = jnp.where(at == 0, 0.0, pltpu.roll(above[rows - group :], 1, 0))
        above = jnp.concatenate([wrap, above[: rows - group]], axis=0)
        wrap = jnp.where(at == group - 1, 0.0, pltpu.roll(below[:group], group - 1, 0))
        below = jnp.concatenate([below[group:], wrap], axis=0)
        blocks.append(here + above + below)
    return blocks


def scale_of(value):
    return lax.rsqrt(jnp.sum(value * value, axis=-1, keepdims=True) * (1.0 / value.shape[-1]) + EPS)


def norm_back(value, gain, grad):
    scale = scale_of(value)
    normed = value * scale
    half = 0.5 * gain
    h = normed * half
    t = jnp.tanh(h)
    d_norm = grad * ((1.0 + t) * (1.0 + h - h * t)) * half
    mean = jnp.sum(d_norm * normed, axis=-1, keepdims=True) * (1.0 / value.shape[-1])
    return scale * (d_norm - normed * mean)


def thirds(value):
    part = value.shape[-1] // 3
    return [value[:, p * part : (p + 1) * part] for p in range(3)]


def two_sums(value):
    left, middle, right = thirds(value)
    first = lax.broadcasted_iota(jnp.int32, middle.shape, 1) < middle.shape[1] // 2
    left = jnp.sum(left + jnp.where(first, middle, 0.0), axis=-1, keepdims=True)
    right = jnp.sum(right + jnp.where(first, 0.0, middle), axis=-1, keepdims=True)
    return left, right, first


def hidden(core, kind, src, gain, hid):
    width = gain.shape[-1]
    part = 2 * width // 3
    gains = thirds(jnp.concatenate([gain, gain], axis=1))
    for frame in range(2):
        for p in range(3):
            lanes = pl.ds(pl.multiple_of((p + core) * 2 * width, 2 * width), 2 * width)
            value = src[kind, frame, :, lanes].astype(F32)
            left, right, first = two_sums(value * value)
            left, right = (0.5 * lax.rsqrt(total * (1.0 / width) + EPS) for total in (left, right))
            scales = left, jnp.where(first, left, right), right
            for n, (piece, scale, g) in enumerate(zip(thirds(value), scales, gains)):
                h = piece * scale * g
                at = p * 2 * width + n * part
                hid[frame, :, at : at + part] = (h + h * jnp.tanh(h)).astype(BF16)


def fields_of(core, kind, src, gain, hid):
    width = gain.shape[-1]
    hidden(core, kind, src, gain, hid)
    lanes = pl.ds(pl.multiple_of(core * 2 * width, 2 * width), 6 * width)
    return [lefts(hid[f], 4, width) for f in range(2)], [lefts(src[1 - kind, f, :, lanes], 4, width) for f in range(2)]


def own_kernel(own, gain_one, conv_one, turned, z_part, d_part, hid):
    rows = own.shape[2]
    xs, gs = fields_of(lax.axis_index("core"), x_core(lax.axis_index("tm"), lax.axis_size("tm")), own, gain_one[...], hid)
    for t, terms in enumerate(([(2, xs[0])], [(1, xs[0]), (2, xs[1])])):
        for c, block in enumerate(conv_sum(terms, conv_one, False, rows)):
            z_part[t, c] = block
    for t, terms in enumerate(([(0, gs[0]), (1, gs[1])], [(0, gs[1])])):
        for c, block in enumerate(conv_sum(terms, turned, True, rows)):
            d_part[t, c] = block


def middle_kernel(
    other, z_part, d_part, two, gain_one, gain_two, conv_one, one, out, send, hid, z_all, d_all
):
    width = gain_one.shape[-1]
    rows = other.shape[2]
    xs, gs = fields_of(lax.axis_index("core"), x_core_other(lax.axis_index("tm"), lax.axis_size("tm")), other, gain_one[...], hid)
    for t, terms in enumerate(([(0, xs[0]), (1, xs[1])], [(0, xs[1])])):
        for c, block in enumerate(conv_sum(terms, conv_one, False, rows)):
            z_all[t, c] = z_part[t, c] + block
    for t, terms in enumerate(([(2, gs[0])], [(1, gs[0]), (2, gs[1])])):
        for c, block in enumerate(conv_sum(terms, two, True, rows)):
            d_all[t, c] = d_part[t, c] + block
    me, last = lax.axis_index(("chip", "core")), lax.axis_size(("chip", "core")) - 1
    outside = {0: me == 0, 3: me == last}

    def back(t):
        for c in range(4):
            d_z = norm_back(z_all[t, c], gain_two[...], d_all[t, c])
            if c in outside:
                d_z = jnp.where(outside[c], 0.0, d_z)
            out[t, :, c * width : (c + 1) * width] = d_z.astype(BF16)
        return lefts(out[t], 2, width)

    def give(t, blocks):
        for c, block in enumerate(blocks):
            send[t, :, c * width : (c + 1) * width] = block.astype(BF16)

    d_first = back(0)
    give(0, conv_sum([(2, d_first)], one, True, rows))
    middle = conv_sum([(1, d_first)], one, True, rows)
    late = conv_sum([(2, back(1))], one, True, rows)
    give(1, [a + b for a, b in zip(middle, late)])


def halves(value):
    left, right, first = two_sums(value)
    shape = first.shape
    pieces = jnp.broadcast_to(left, shape), jnp.where(first, left, right), jnp.broadcast_to(right, shape)
    return jnp.concatenate(pieces, axis=1)


def early_kernel(own, d_own, one, gain_one, base, slope, along, across, d_all):
    width = gain_one.shape[-1]
    rows = own.shape[2]
    ds = [lefts(d_own[f], 2, width) for f in range(2)]
    for t, terms in enumerate(([(0, ds[0]), (1, ds[1])], [(0, ds[1])])):
        for c, block in enumerate(conv_sum(terms, one, True, rows)):
            d_all[t, :, c * width : (c + 1) * width] = block
    lanes = pl.ds(pl.multiple_of((1 + lax.axis_index("core")) * 2 * width, 2 * width), 2 * width)
    gain = jnp.concatenate([gain_one[...]] * 2, axis=1)
    kind = x_core(lax.axis_index("tm"), lax.axis_size("tm"))
    for t in range(2):
        value = own[kind, t, :, lanes].astype(F32)
        scale = lax.rsqrt(halves(value * value) * (1.0 / width) + EPS)
        normed = value * scale
        h = normed * (0.5 * gain)
        bend = jnp.tanh(h)
        turn = (1.0 + bend) * (1.0 + h - h * bend) * (0.5 * gain)
        slope[t] = scale * turn
        along[t] = scale * normed * (1.0 / width)
        across[t] = turn * normed
        grad = d_all[t]
        total = halves(across[t] * grad)
        base[t] = own[1 - kind, t, :, lanes].astype(F32) + slope[t] * grad - along[t] * total


def last_kernel(late, base, slope, along, across, out, natural):
    rows = out.shape[1]
    group = rows // 8
    for t in range(2):
        grad = late[t].astype(F32)
        result = base[t] + slope[t] * grad - along[t] * halves(across[t] * grad)
        for p in range(natural.shape[0]):
            for r in range(8):
                piece = result[r * group : (r + 1) * group, p * 128 : (p + 1) * 128]
                natural[p, pl.ds(r, group, stride=8), :] = piece
        for p in range(natural.shape[0]):
            out[t, :, p * 128 : (p + 1) * 128] = natural[p].astype(BF16)


def call(kernel, ins, outs, scratch, flops, *args, limit=16 * MIB, to="v"):
    kinds = {"v": pltpu.VMEM, "s": pltpu.SMEM, "h": pltpu.HBM}
    return pl.pallas_call(
        kernel,
        out_shape=outs,
        in_specs=[pl.BlockSpec(memory_space=kinds[kind]) for kind in ins],
        out_specs=jax.tree.map(lambda _: pl.BlockSpec(memory_space=kinds[to]), outs),
        scratch_shapes=scratch,
        compiler_params=pltpu.CompilerParams(vmem_limit_bytes=limit),
        cost_estimate=pl.CostEstimate(flops=flops, bytes_accessed=4 << 20, transcendentals=0),
    )(*args)


def body(inputs, cotangent, frame_weight, gain_one, conv_one, gain_two, conv_two):
    tiles = lax.axis_size(("chip", "core"))
    frames, _, merged = inputs.shape
    width = gain_one.shape[0]
    wide = 8 * width
    gain_one, gain_two = gain_one.reshape(1, width), gain_two.reshape(1, width)
    array = jax.ShapeDtypeStruct
    one = 2 * tiles * 9 * width * width

    local = [pltpu.SMEM((frames,), jnp.int32)] + [pltpu.VMEM((frames, merged), BF16)] * 2
    local += [pltpu.VMEM((tiles // 2, frames, wide), BF16)] * 2
    blocks = call(
        pack_kernel, "hhh", array((tiles // 2, 2, frames, wide), BF16), local + [pltpu.SemaphoreType.DMA((5,))], 10**6,
        frame_weight, inputs.reshape(frames, merged), cotangent.reshape(frames, merged), limit=60 * MIB, to="h",
    ).reshape(tiles, frames, wide)
    held = lax.all_to_all(blocks, ("chip", "core"), 0, 0)
    held = held.reshape(tiles // 8, 8, frames, wide).transpose(2, 1, 0, 3).reshape(frames, tiles, wide)
    turned = array((3, 3, width, 3 * width), BF16)
    turned_two = call(turn_kernel, "v", turned, [], 10**9, conv_two)
    held, turned_two = lax.optimization_barrier((held, turned_two))
    arrived = jnp.concatenate([spread(held[frame : frame + 1]) for frame in range(frames)], axis=0)
    own = lax.all_gather(held, "core")
    turned_one = call(turn_kernel, "v", turned, [], 10**9, conv_one)
    sums = (frames, 4, tiles, width)
    hid = pltpu.VMEM((frames, tiles, 6 * width), BF16)
    z_part, d_part = call(
        own_kernel, "vvvv", (array(sums, F32), array(sums, F32)), [hid], 24 * one,
        own, gain_one, conv_one, turned_two,
    )
    other = lax.all_gather(arrived, "core")
    d_own, send = call(
        middle_kernel, "vvvvvvvv",
        (array((frames, tiles, 4 * width), BF16), array((frames, tiles, 2 * width), BF16)),
        [hid, pltpu.VMEM(sums, F32), pltpu.VMEM(sums, F32)], 24 * one,
        other, z_part, d_part, turned_two, gain_one, gain_two, conv_one, turned_one,
    )
    late = shifted(send, "tm", -1)
    field = (frames, tiles, 2 * width)
    parts = call(
        early_kernel, "vvvv", (array(field, F32),) * 4, [pltpu.VMEM(field, F32)], 6 * one,
        own, d_own, turned_one, gain_one,
    )
    natural = pltpu.VMEM((2 * width // 128, tiles, 128), F32)
    return call(last_kernel, "vvvvv", array(field, BF16), [natural], one, late, *parts)


def solution(mesh):
    tm, tile = mesh.devices.shape
    chips = Mesh(mesh.devices.reshape(tm, tile // 2, 2), ("tm", "chip", "core"))
    tiles = ("chip", "core")
    in_specs = (P("tm", tiles, None), P("tm", tiles, None), P("tm"), P(), P(), P(), P())
    out_specs = P("tm", None, tiles)
    return jax.shard_map(body, mesh=chips, in_specs=in_specs, out_specs=out_specs, check_vma=False)
```

```python
import jax
import jax.numpy as jnp
from jax import lax
from jax.experimental import pallas as pl
from jax.experimental.pallas import tpu as pltpu
from jax.sharding import Mesh
from jax.sharding import PartitionSpec as P

EPS = 1e-06
F32, BF16 = jnp.float32, jnp.bfloat16
MIB = 1024 * 1024


def shifted(value, axis, steps):
    count = lax.axis_size(axis)
    first, last = (max(0, -steps), min(count, count - steps))
    return lax.ppermute(value, axis, [(source, source + steps) for source in range(first, last)])


def spread(value):
    count = lax.axis_size("tm")
    later = [(2 * k, 2 * k + 2) for k in range(count - 1)]
    earlier = [(2 * k + 3, 2 * k + 1) for k in range(count - 1)]
    return lax.ppermute(value, ("tm", "core"), later + earlier)


def pack_kernel(weight, x, c, out, scale, x_here, dy, x_blocks, dy_blocks, sems):
    chips, _, frames, wide = out.shape
    pair = wide // 4
    moves = [
        pltpu.make_async_copy(src, dst, sems.at[n])
        for n, (src, dst) in enumerate(((x, x_here), (c, dy), (weight, scale)))
    ]
    for move in moves:
        move.start()

    def lay(src, blocks, kind):
        none = jnp.zeros((frames, pair), BF16)
        blocks[0, :, :pair] = none
        blocks[chips - 1, :, 3 * pair :] = none
        for q in range(chips):
            first, last = max(0, 2 * q - 1), min(2 * chips, 2 * q + 3)
            skip = first - (2 * q - 1)
            blocks[q, :, skip * pair : (skip + last - first) * pair] = src[:, first * pair : last * pair]
        move = pltpu.make_async_copy(blocks, out.at[:, kind], sems.at[3 + kind])
        move.start()
        return move

    moves[0].wait()
    x_move = lay(x_here, x_blocks, 0)
    moves[1].wait()
    moves[2].wait()
    at = lax.broadcasted_iota(jnp.int32, dy.shape, 0)
    factor = jnp.where(at == 0, scale[0].astype(F32), scale[1].astype(F32)).astype(BF16)
    dy[...] = dy[...] * factor
    dy_move = lay(dy, dy_blocks, 1)
    x_move.wait()
    dy_move.wait()


def turn_kernel(src, dst):
    width = src.shape[-1]
    for a in range(3):
        for b in range(3):
            for e in range(3):
                dst[a, b, :, e * width : (e + 1) * width] = src[2 - a, 2 - b, 2 - e]


def lefts(field, columns, width):
    odd = field[:, width:]
    parts = []
    for c in range(columns):
        src, at = (field, c) if c % 2 == 0 else (odd, c - 1)
        parts.append(src[:, at * width : (at + 3) * width])
    return jnp.concatenate(parts, axis=0)


def conv_sum(terms, kern, flipped, rows):
    dims = (((1,), (1 if flipped else 0,)), ((), ()))
    taps = []
    for b in range(3):
        total = None
        for a, left in terms:
            right = kern[a, b]
            if not flipped:
                right = right.reshape(left.shape[1], right.shape[-1])
            part = lax.dot_general(left, right, dims, preferred_element_type=F32)
            total = part if total is None else total + part
        taps.append(total)
    group = rows // 8
    at = lax.broadcasted_iota(jnp.int32, (group, taps[0].shape[1]), 0)
    blocks = []
    for first in range(0, taps[0].shape[0], rows):
        above, here, below = (tap[first : first + rows] for tap in taps)
        wrap = jnp.where(at == 0, 0.0, pltpu.roll(above[rows - group :], 1, 0))
        above = jnp.concatenate([wrap, above[: rows - group]], axis=0)
        wrap = jnp.where(at == group - 1, 0.0, pltpu.roll(below[:group], group - 1, 0))
        below = jnp.concatenate([below[group:], wrap], axis=0)
        blocks.append(here + above + below)
    return blocks


def scale_of(value):
    return lax.rsqrt(jnp.sum(value * value, axis=-1, keepdims=True) * (1.0 / value.shape[-1]) + EPS)


def norm_back(value, gain, grad):
    scale = scale_of(value)
    normed = value * scale
    half = 0.5 * gain
    h = normed * half
    t = jnp.tanh(h)
    d_norm = grad * ((1.0 + t) * (1.0 + h - h * t)) * half
    mean = jnp.sum(d_norm * normed, axis=-1, keepdims=True) * (1.0 / value.shape[-1])
    return scale * (d_norm - normed * mean)


def thirds(value):
    part = value.shape[-1] // 3
    return [value[:, p * part : (p + 1) * part] for p in range(3)]


def two_sums(value):
    left, middle, right = thirds(value)
    first = lax.broadcasted_iota(jnp.int32, middle.shape, 1) < middle.shape[1] // 2
    left = jnp.sum(left + jnp.where(first, middle, 0.0), axis=-1, keepdims=True)
    right = jnp.sum(right + jnp.where(first, 0.0, middle), axis=-1, keepdims=True)
    return left, right, first


def hidden(core, src, gain, hid):
    width = gain.shape[-1]
    part = 2 * width // 3
    gains = thirds(jnp.concatenate([gain, gain], axis=1))
    for frame in range(2):
        for p in range(3):
            lanes = pl.ds(pl.multiple_of((p + core) * 2 * width, 2 * width), 2 * width)
            value = src[0, frame, :, lanes].astype(F32)
            left, right, first = two_sums(value * value)
            left, right = (0.5 * lax.rsqrt(total * (1.0 / width) + EPS) for total in (left, right))
            scales = left, jnp.where(first, left, right), right
            for n, (piece, scale, g) in enumerate(zip(thirds(value), scales, gains)):
                h = piece * scale * g
                at = p * 2 * width + n * part
                hid[frame, :, at : at + part] = (h + h * jnp.tanh(h)).astype(BF16)


def fields_of(core, src, gain, hid):
    width = gain.shape[-1]
    hidden(core, src, gain, hid)
    lanes = pl.ds(pl.multiple_of(core * 2 * width, 2 * width), 6 * width)
    return [lefts(hid[f], 4, width) for f in range(2)], [lefts(src[1, f, :, lanes], 4, width) for f in range(2)]


def own_kernel(own, gain_one, conv_one, turned, z_part, d_part, hid):
    rows = own.shape[2]
    xs, gs = fields_of(lax.axis_index("core"), own, gain_one[...], hid)
    for t, terms in enumerate(([(2, xs[0])], [(1, xs[0]), (2, xs[1])])):
        for c, block in enumerate(conv_sum(terms, conv_one, False, rows)):
            z_part[t, c] = block
    for t, terms in enumerate(([(0, gs[0]), (1, gs[1])], [(0, gs[1])])):
        for c, block in enumerate(conv_sum(terms, turned, True, rows)):
            d_part[t, c] = block


def middle_kernel(
    other, z_part, d_part, two, gain_one, gain_two, conv_one, one, out, send, hid, z_all, d_all
):
    width = gain_one.shape[-1]
    rows = other.shape[2]
    xs, gs = fields_of(lax.axis_index("core"), other, gain_one[...], hid)
    for t, terms in enumerate(([(0, xs[0]), (1, xs[1])], [(0, xs[1])])):
        for c, block in enumerate(conv_sum(terms, conv_one, False, rows)):
            z_all[t, c] = z_part[t, c] + block
    for t, terms in enumerate(([(2, gs[0])], [(1, gs[0]), (2, gs[1])])):
        for c, block in enumerate(conv_sum(terms, two, True, rows)):
            d_all[t, c] = d_part[t, c] + block
    me, last = lax.axis_index(("chip", "core")), lax.axis_size(("chip", "core")) - 1
    outside = {0: me == 0, 3: me == last}

    def back(t):
        for c in range(4):
            d_z = norm_back(z_all[t, c], gain_two[...], d_all[t, c])
            if c in outside:
                d_z = jnp.where(outside[c], 0.0, d_z)
            out[t, :, c * width : (c + 1) * width] = d_z.astype(BF16)
        return lefts(out[t], 2, width)

    def give(t, blocks):
        for c, block in enumerate(blocks):
            send[t, :, c * width : (c + 1) * width] = block.astype(BF16)

    d_first = back(0)
    give(0, conv_sum([(2, d_first)], one, True, rows))
    middle = conv_sum([(1, d_first)], one, True, rows)
    late = conv_sum([(2, back(1))], one, True, rows)
    give(1, [a + b for a, b in zip(middle, late)])


def halves(value):
    left, right, first = two_sums(value)
    shape = first.shape
    pieces = jnp.broadcast_to(left, shape), jnp.where(first, left, right), jnp.broadcast_to(right, shape)
    return jnp.concatenate(pieces, axis=1)


def early_kernel(own, d_own, one, gain_one, base, slope, along, across, d_all):
    width = gain_one.shape[-1]
    rows = own.shape[2]
    ds = [lefts(d_own[f], 2, width) for f in range(2)]
    for t, terms in enumerate(([(0, ds[0]), (1, ds[1])], [(0, ds[1])])):
        for c, block in enumerate(conv_sum(terms, one, True, rows)):
            d_all[t, :, c * width : (c + 1) * width] = block
    lanes = pl.ds(pl.multiple_of((1 + lax.axis_index("core")) * 2 * width, 2 * width), 2 * width)
    gain = jnp.concatenate([gain_one[...]] * 2, axis=1)
    for t in range(2):
        value = own[0, t, :, lanes].astype(F32)
        scale = lax.rsqrt(halves(value * value) * (1.0 / width) + EPS)
        normed = value * scale
        h = normed * (0.5 * gain)
        bend = jnp.tanh(h)
        turn = (1.0 + bend) * (1.0 + h - h * bend) * (0.5 * gain)
        slope[t] = scale * turn
        along[t] = scale * normed * (1.0 / width)
        across[t] = turn * normed
        grad = d_all[t]
        total = halves(across[t] * grad)
        base[t] = own[1, t, :, lanes].astype(F32) + slope[t] * grad - along[t] * total


def last_kernel(late, base, slope, along, across, out, natural):
    rows = out.shape[1]
    group = rows // 8
    for t in range(2):
        grad = late[t].astype(F32)
        result = base[t] + slope[t] * grad - along[t] * halves(across[t] * grad)
        for p in range(natural.shape[0]):
            for r in range(8):
                piece = result[r * group : (r + 1) * group, p * 128 : (p + 1) * 128]
                natural[p, pl.ds(r, group, stride=8), :] = piece
        for p in range(natural.shape[0]):
            out[t, :, p * 128 : (p + 1) * 128] = natural[p].astype(BF16)


def call(kernel, ins, outs, scratch, flops, *args, limit=16 * MIB, to="v"):
    kinds = {"v": pltpu.VMEM, "s": pltpu.SMEM, "h": pltpu.HBM}
    return pl.pallas_call(
        kernel,
        out_shape=outs,
        in_specs=[pl.BlockSpec(memory_space=kinds[kind]) for kind in ins],
        out_specs=jax.tree.map(lambda _: pl.BlockSpec(memory_space=kinds[to]), outs),
        scratch_shapes=scratch,
        compiler_params=pltpu.CompilerParams(vmem_limit_bytes=limit),
        cost_estimate=pl.CostEstimate(flops=flops, bytes_accessed=4 << 20, transcendentals=0),
    )(*args)


def body(inputs, cotangent, frame_weight, gain_one, conv_one, gain_two, conv_two):
    tiles = lax.axis_size(("chip", "core"))
    frames, _, merged = inputs.shape
    width = gain_one.shape[0]
    wide = 8 * width
    gain_one, gain_two = gain_one.reshape(1, width), gain_two.reshape(1, width)
    array = jax.ShapeDtypeStruct
    one = 2 * tiles * 9 * width * width

    local = [pltpu.SMEM((frames,), jnp.int32)] + [pltpu.VMEM((frames, merged), BF16)] * 2
    local += [pltpu.VMEM((tiles // 2, frames, wide), BF16)] * 2
    blocks = call(
        pack_kernel, "hhh", array((tiles // 2, 2, frames, wide), BF16), local + [pltpu.SemaphoreType.DMA((5,))], 10**6,
        frame_weight, inputs.reshape(frames, merged), cotangent.reshape(frames, merged), limit=60 * MIB, to="h",
    ).reshape(tiles, frames, wide)
    held = lax.all_to_all(blocks, ("chip", "core"), 0, 0)
    held = held.reshape(tiles // 8, 8, frames, wide).transpose(2, 1, 0, 3).reshape(frames, tiles, wide)
    turned = array((3, 3, width, 3 * width), BF16)
    turned_two = call(turn_kernel, "v", turned, [], 10**9, conv_two)
    held, turned_two = lax.optimization_barrier((held, turned_two))
    arrived = spread(held)
    own = lax.all_gather(held, "core")
    turned_one = call(turn_kernel, "v", turned, [], 10**9, conv_one)
    sums = (frames, 4, tiles, width)
    hid = pltpu.VMEM((frames, tiles, 6 * width), BF16)
    z_part, d_part = call(
        own_kernel, "vvvv", (array(sums, F32), array(sums, F32)), [hid], 24 * one,
        own, gain_one, conv_one, turned_two,
    )
    other = lax.all_gather(arrived, "core")
    d_own, send = call(
        middle_kernel, "vvvvvvvv",
        (array((frames, tiles, 4 * width), BF16), array((frames, tiles, 2 * width), BF16)),
        [hid, pltpu.VMEM(sums, F32), pltpu.VMEM(sums, F32)], 24 * one,
        other, z_part, d_part, turned_two, gain_one, gain_two, conv_one, turned_one,
    )
    late = shifted(send, "tm", -1)
    field = (frames, tiles, 2 * width)
    parts = call(
        early_kernel, "vvvv", (array(field, F32),) * 4, [pltpu.VMEM(field, F32)], 6 * one,
        own, d_own, turned_one, gain_one,
    )
    natural = pltpu.VMEM((2 * width // 128, tiles, 128), F32)
    return call(last_kernel, "vvvvv", array(field, BF16), [natural], one, late, *parts)


def solution(mesh):
    tm, tile = mesh.devices.shape
    chips = Mesh(mesh.devices.reshape(tm, tile // 2, 2), ("tm", "chip", "core"))
    tiles = ("chip", "core")
    in_specs = (P("tm", tiles, None), P("tm", tiles, None), P("tm"), P(), P(), P(), P())
    out_specs = P("tm", None, tiles)
    return jax.shard_map(body, mesh=chips, in_specs=in_specs, out_specs=out_specs, check_vma=False)
```
